256 devices in a mesh: gx: 32 (over z_hi, y, core), gy: 8 (over z_lo, x).
Axes of the slice: x: 4, y: 4, z: 8 (z_hi: 4, z_lo: 2; z = z_hi * 2 + z_lo), core: 2. Of those that a mesh axis runs over, the one named last changes fastest.
Arguments:
- tokens: bfloat16 [256, 16384], P('gy', 'gx'), may hold values from -6 to 6
- gate_payload: bfloat16 [16384, 26624], P('gx', 'gy'), may hold values from -0.09375 to 0.09375
- gate_scales: float32 [128, 208], P('gx', 'gy'), may hold values from 0.5 to 2
- up_payload: bfloat16 [16384, 26624], P('gx', 'gy'), may hold values from -0.046875 to 0.046875
- up_scales: float32 [128, 208], P('gx', 'gy'), may hold values from 0.5 to 2
- down_payload: bfloat16 [26624, 16384], P('gy', 'gx'), may hold values from -0.0390625 to 0.0390625
- down_scales: float32 [208, 128], P('gy', 'gx'), may hold values from 0.5 to 2
Outputs:
- mixed: bfloat16 [256, 16384], P('gy', 'gx')
The draws below stay inside these ranges and needn't reach their ends.
All inputs are finite; a program needn't handle non-finite values.
Results may differ from the reference program's by a relative error of at most 0.007.
Values may be sent and summed in bfloat16 or wider, within the bound.
No kernel may reach another device: no remote copies, remote signals or barrier semaphores. Data moves between devices by JAX's collectives and lax.ppermute only.
A program may use at most 64 MiB of HBM per device.

```python
import math
import jax
import jax.numpy as jnp
from jax import lax

D = 16384
FF = 26624
BLOCK = 128
TOKENS = 256


def spiked(result, key, source, target, shards_of, factor):
    owner, partner = [(jnp.arange(result.shape[dim]) // (result.shape[dim] // shards_of)).reshape([-1 if axis == dim else 1 for axis in range(result.ndim)]) for dim in (source, target)]
    chosen = jax.random.permutation(key, shards_of)[partner]
    strong = (owner == chosen) | (owner == (partner + shards_of // 2) % shards_of)
    return jnp.where(strong, factor * result, result)


def block_levels(rng, extent, shards, smallest, high):
    factor_of = 1.0
    for position, parts in shards:
        heights = jax.random.uniform(jax.random.fold_in(jax.random.fold_in(rng, 6), position), (parts,), jnp.float32, smallest / len(shards), high / len(shards))
        factor_of = factor_of * jnp.repeat(jnp.exp(heights), extent[position] // parts).reshape((-1,) + (1,) * (len(extent) - 1 - position))
    return factor_of


def centred(stream_key, dims, width, limit, cuts=(), dtype=jnp.bfloat16):
    result = width * jax.random.normal(stream_key, dims, jnp.float32)
    if cuts:
        result = result * block_levels(stream_key, dims, cuts, -0.22, 0.18)
    return jnp.clip(result, -limit, limit).astype(dtype)


def gaussian_with(stream_key, extent, scale, reach, shards, heavy, kind=jnp.bfloat16):
    entries = scale * jax.random.normal(stream_key, extent, jnp.float32)
    if shards:
        entries = entries * block_levels(stream_key, extent, shards, -0.22, 0.18)
    return jnp.clip(spiked(entries, jax.random.fold_in(stream_key, 3), *heavy), -reach, reach).astype(kind)


def setup_inputs(seed: int = 0) -> dict:
    key_of = jax.random.split(jax.random.key(seed), 8)
    return {
        "tokens": gaussian_with(key_of[0], (TOKENS, D), 1.0, 6.0, ((0, 8), (1, 32)), (1, 0, 32, 2.75)),
        "gate_payload": gaussian_with(key_of[1], (D, FF), D ** -0.5, 0.09375, ((0, 32), (1, 8)), (0, 1, 32, 2.75)),
        "gate_scales": jnp.clip(jnp.exp(math.log(2.0) - 1.3862944 * jax.random.uniform(key_of[2], (D // BLOCK, FF // BLOCK), jnp.float32) ** block_levels(key_of[2], (D // BLOCK, FF // BLOCK), ((0, 32), (1, 8)), -0.2, 0.2)), 0.5, 2.0),
        "up_payload": centred(key_of[3], (D, FF), D ** -0.5, 0.046875, ((0, 32), (1, 8))),
        "up_scales": jnp.clip(jnp.exp(math.log(2.0) - 1.3862944 * jax.random.uniform(key_of[4], (D // BLOCK, FF // BLOCK), jnp.float32) ** block_levels(key_of[4], (D // BLOCK, FF // BLOCK), ((0, 32), (1, 8)), -0.2, 0.2)), 0.5, 2.0),
        "down_payload": centred(key_of[5], (FF, D), FF ** -0.5, 0.0390625, ((0, 8), (1, 32))),
        "down_scales": jnp.clip(jnp.exp(math.log(2.0) - 1.3862944 * jax.random.uniform(key_of[6], (FF // BLOCK, D // BLOCK), jnp.float32) ** block_levels(key_of[6], (FF // BLOCK, D // BLOCK), ((0, 8), (1, 32)), -0.2, 0.2)), 0.5, 2.0),
    }


def dequantize(payload, scales):
    row_count, col_count = payload.shape
    blocked = payload.reshape(row_count // BLOCK, BLOCK, col_count // BLOCK, BLOCK).astype(jnp.float32)
    blocked = blocked * scales[:, None, :, None]
    return blocked.reshape(row_count, col_count).astype(jnp.bfloat16)


def reference(tokens, gate_payload, gate_scales, up_payload, up_scales, down_payload, down_scales):
    part_width = FF // 8
    part_blocks = part_width // BLOCK

    def one_part(index, accumulated):
        start = index * part_width
        block_start = index * part_blocks
        gate_weight = dequantize(lax.dynamic_slice_in_dim(gate_payload, start, part_width, 1),
                                 lax.dynamic_slice_in_dim(gate_scales, block_start, part_blocks, 1))
        up_weight = dequantize(lax.dynamic_slice_in_dim(up_payload, start, part_width, 1),
                               lax.dynamic_slice_in_dim(up_scales, block_start, part_blocks, 1))
        down_weight = dequantize(lax.dynamic_slice_in_dim(down_payload, start, part_width, 0),
                                 lax.dynamic_slice_in_dim(down_scales, block_start, part_blocks, 0))
        gate = jnp.dot(tokens, gate_weight, preferred_element_type=jnp.float32)
        up = jnp.dot(tokens, up_weight, preferred_element_type=jnp.float32)
        hidden = (jax.nn.silu(gate) * up).astype(jnp.bfloat16)
        return accumulated + jnp.dot(hidden, down_weight, preferred_element_type=jnp.float32)

    initial = jnp.zeros((tokens.shape[0], D), jnp.float32)
    summed = lax.fori_loop(0, 8, one_part, initial)
    return summed.astype(jnp.bfloat16)
```

```python
import jax
import jax.numpy as jnp
from jax import lax
from jax.experimental import pallas as pl
from jax.experimental.pallas import tpu as pltpu
from jax.sharding import PartitionSpec as P

BLOCK = 128
F32 = jnp.float32
BF16 = jnp.bfloat16
NZ, NY, NC, NG = 4, 4, 2, 8


def gx_pairs(dz, dy, dc):
    pairs = []
    for z in range(NZ):
        for y in range(NY):
            for c in range(NC):
                src = (z * NY + y) * NC + c
                dst = (((z + dz) % NZ) * NY + (y + dy) % NY) * NC + (c + dc) % NC
                pairs.append((src, dst))
    return pairs


def move_gx(x, dz=0, dy=0, dc=0):
    return lax.ppermute(x, "gx", gx_pairs(dz, dy, dc))


def move_gy(x, k):
    return lax.ppermute(x, "gy", [(i, (i + k) % NG) for i in range(NG)])


def scaled(payload, scale):
    return (payload.astype(F32) * scale).astype(BF16)


def pair_kernel(half, gate, up, gate_scales, up_scales, out):
    column = half[0] * pl.num_programs(0) + pl.program_id(0)
    for row in range(gate.shape[0] // BLOCK):
        rows = slice(row * BLOCK, (row + 1) * BLOCK)
        out[rows, :BLOCK] = scaled(gate[rows, :], gate_scales[row, column])
        out[rows, BLOCK:] = scaled(up[rows, :], up_scales[row, column])


def pair_weights(half, gate, gate_scales, up, up_scales):
    rows, columns = gate.shape
    blocks = columns // (2 * BLOCK)
    weight = pl.BlockSpec((rows, BLOCK), lambda i, h: (0, h[0] * blocks + i))
    scales = pl.BlockSpec(memory_space=pltpu.SMEM)
    return pl.pallas_call(
        pair_kernel,
        out_shape=jax.ShapeDtypeStruct((rows, columns), BF16),
        grid_spec=pltpu.PrefetchScalarGridSpec(
            num_scalar_prefetch=1,
            grid=(blocks,),
            in_specs=[weight, weight, scales, scales],
            out_specs=pl.BlockSpec((rows, 2 * BLOCK), lambda i, h: (0, i)),
        ),
        cost_estimate=pl.CostEstimate(
            flops=2 * rows * columns, bytes_accessed=4 * rows * columns, transcendentals=0
        ),
    )(half, gate, up, gate_scales, up_scales)


def down_kernel(half, payload, scales, out):
    base = half[0] * (payload.shape[0] // BLOCK)
    column = pl.program_id(0)
    for row in range(payload.shape[0] // BLOCK):
        rows = slice(row * BLOCK, (row + 1) * BLOCK)
        out[rows, :] = scaled(payload[rows, :], scales[base + row, column])


def down_weights(half, payload, scales):
    rows, columns = payload.shape
    rows //= 2
    return pl.pallas_call(
        down_kernel,
        out_shape=jax.ShapeDtypeStruct((rows, columns), BF16),
        grid_spec=pltpu.PrefetchScalarGridSpec(
            num_scalar_prefetch=1,
            grid=(columns // BLOCK,),
            in_specs=[
                pl.BlockSpec((rows, BLOCK), lambda i, h: (h[0], i)),
                pl.BlockSpec(memory_space=pltpu.SMEM),
            ],
            out_specs=pl.BlockSpec((rows, BLOCK), lambda i, h: (0, i)),
        ),
        cost_estimate=pl.CostEstimate(
            flops=rows * columns, bytes_accessed=4 * rows * columns, transcendentals=0
        ),
    )(half, payload, scales)


def turned(x, y, z):
    x = lax.dynamic_slice_in_dim(jnp.concatenate([x, x], 0), y, NY, 0)
    return lax.dynamic_slice_in_dim(jnp.concatenate([x, x], 1), z, NZ, 1)


def dot(a, b):
    return lax.dot_general(a, b, (((1,), (0,)), ((), ())), preferred_element_type=F32)


def local(tokens, gate_payload, gate_scales, up_payload, up_scales, down_payload, down_scales):
    index = lax.axis_index("gx")
    z, y, c = index // (NY * NC), (index // NC) % NY, index % NC
    mine = jnp.reshape(c, (1,)).astype(jnp.int32)
    other = 1 - mine

    blocks = [tokens] + [move_gy(tokens, k) for k in range(1, NG)]
    w_other = pair_weights(other, gate_payload, gate_scales, up_payload, up_scales)
    w_mine = pair_weights(mine, gate_payload, gate_scales, up_payload, up_scales)
    d_mine = down_weights(mine, down_payload, down_scales)
    d_other = down_weights(other, down_payload, down_scales)

    width = tokens.shape[1]
    features = jnp.concatenate(blocks, axis=0)
    count = features.shape[0]
    part = count // (NY * NZ)
    features = turned(features.reshape(NY, NZ, part, width), y, z).reshape(count, width)

    received = move_gx(dot(features, w_other).astype(BF16), dc=1)
    total = dot(features, w_mine) + received.astype(F32)

    for steps, kind in ((NY, "dy"), (NZ, "dz")):
        rows = total.shape[0] // steps
        parts = [
            move_gx(total[k * rows : (k + 1) * rows].astype(BF16), **{kind: k})
            for k in range(1, steps)
        ]
        total = total[:rows]
        for piece in parts:
            total = total + piece.astype(F32)

    pairs = total.reshape(part, -1, 2, BLOCK)
    hidden = (jax.nn.silu(pairs[:, :, 0]) * pairs[:, :, 1]).astype(BF16).reshape(part, -1)

    for steps, kind in ((NZ, "dz"), (NY, "dy")):
        hidden = jnp.concatenate(
            [hidden] + [move_gx(hidden, **{kind: -k}) for k in range(1, steps)], axis=0
        )
    theirs = move_gx(hidden, dc=1)
    terms = dot(hidden, d_mine) + dot(theirs, d_other)

    terms = turned(terms.reshape(NY, NZ, part, -1), (NY - y) % NY, (NZ - z) % NZ)
    terms = terms.reshape(NG, count // NG, -1)
    result = terms[0]
    for piece in [move_gy(terms[k].astype(BF16), NG - k) for k in range(1, NG)]:
        result = result + piece.astype(F32)
    return result.astype(BF16)


def solution(mesh):
    placed = (
        P("gy", "gx"),
        P("gx", "gy"),
        P("gx", "gy"),
        P("gx", "gy"),
        P("gx", "gy"),
        P("gy", "gx"),
        P("gy", "gx"),
    )
    return jax.shard_map(
        local, mesh=mesh, in_specs=placed, out_specs=P("gy", "gx"), check_vma=False
    )
```

```python
import jax
import jax.numpy as jnp
from jax import lax
from jax.experimental import pallas as pl
from jax.experimental.pallas import tpu as pltpu
from jax.sharding import PartitionSpec as P

BLOCK = 128
F32 = jnp.float32
BF16 = jnp.bfloat16
NZ, NY, NC, NL, NX = 4, 4, 2, 2, 4
ROWS = 8
SMEM = pl.BlockSpec(memory_space=pltpu.SMEM)
VMEM = pl.BlockSpec(memory_space=pltpu.VMEM)
HBM = pl.BlockSpec(memory_space=pltpu.HBM)
MIB = 2**20


def move_gx(x, dz=0, dy=0, dc=0):
    pairs = []
    for z in range(NZ):
        for y in range(NY):
            for c in range(NC):
                src = (z * NY + y) * NC + c
                dst = (((z + dz) % NZ) * NY + (y + dy) % NY) * NC + (c + dc) % NC
                pairs.append((src, dst))
    return lax.ppermute(x, "gx", pairs)


def move_gy(x, dl=0, dx=0):
    pairs = []
    for l in range(NL):
        for i in range(NX):
            pairs.append((l * NX + i, (l + dl) % NL * NX + (i + dx) % NX))
    return lax.ppermute(x, "gy", pairs)


def after(x, *others):
    return lax.optimization_barrier((x, *others))[0]


def in_vmem(x):
    return pltpu.with_memory_space_constraint(x, pltpu.VMEM)


def local_call(kernel, outs, *arrays, scalars=(), scratch=(), limit=8, flops=0):
    moved = sum(a.size * a.dtype.itemsize for a in arrays)
    return pl.pallas_call(
        kernel,
        in_specs=[SMEM] * len(scalars) + [VMEM] * len(arrays),
        out_specs=[VMEM] * len(outs),
        out_shape=[pltpu.VMEM(shape, dtype) for shape, dtype in outs],
        scratch_shapes=list(scratch),
        compiler_params=pltpu.CompilerParams(vmem_limit_bytes=limit * MIB),
        cost_estimate=pl.CostEstimate(flops=flops, bytes_accessed=moved, transcendentals=0),
    )(*scalars, *[in_vmem(a) for a in arrays])


def weights_kernel(steps, payload, scales, out, held, sems):
    rows = payload.shape[0] // steps
    copies = [
        pltpu.make_async_copy(
            payload.at[pl.ds(i * rows, rows)], held.at[pl.ds(i * rows, rows)], sems.at[i]
        )
        for i in range(steps)
    ]
    for copy in copies:
        copy.start()
    for i, copy in enumerate(copies):
        copy.wait()
        for row in range(i * rows // BLOCK, (i + 1) * rows // BLOCK):
            for col in range(payload.shape[1] // BLOCK):
                at = (
                    slice(row * BLOCK, (row + 1) * BLOCK),
                    slice(col * BLOCK, (col + 1) * BLOCK),
                )
                out[at] = (held[at].astype(F32) * scales[row, col]).astype(BF16)


def weights(payload, scales, steps):
    rows, cols = payload.shape
    return pl.pallas_call(
        lambda *refs: weights_kernel(steps, *refs),
        in_specs=[HBM, SMEM],
        out_specs=VMEM,
        out_shape=pltpu.VMEM((rows, cols), BF16),
        scratch_shapes=[pltpu.VMEM((rows, cols), BF16), pltpu.SemaphoreType.DMA((steps,))],
        compiler_params=pltpu.CompilerParams(vmem_limit_bytes=16 * MIB),
        cost_estimate=pl.CostEstimate(
            flops=rows * cols, bytes_accessed=4 * rows * cols, transcendentals=0
        ),
    )(pltpu.with_memory_space_constraint(payload, pltpu.HBM), scales)


def join_kernel(*refs):
    *pieces, out = refs
    at = 0
    for piece in pieces:
        rows = piece.shape[0]
        out[at : at + rows, :] = piece[...]
        at += rows


def join(*pieces):
    shape = (sum(p.shape[0] for p in pieces), pieces[0].shape[1])
    return local_call(join_kernel, [(shape, BF16)], *pieces)[0]


def order_kernel(where, out):
    row = lax.broadcasted_iota(jnp.int32, out.shape, 0)
    column = lax.broadcasted_iota(jnp.int32, out.shape, 1)
    block, inner = row // ROWS, row % ROWS
    c, y, z = block // (NY * NZ), block // NZ % NY, block % NZ
    c, y, z = (where[0] + c) % NC, (where[1] + y) % NY, (where[2] + z) % NZ
    chosen = ((c * NY + y) * NZ + z) * ROWS + inner
    out[...] = jnp.where(chosen == column, 1.0, 0.0).astype(BF16)


def turned_row(place, where):
    c, y, z = place // (NY * NZ), place // NZ % NY, place % NZ
    c, y, z = (where[0] + c) % NC, (where[1] + y) % NY, (where[2] + z) % NZ
    return pl.multiple_of(((c * NY + y) * NZ + z) * ROWS, ROWS)


def first_kernel(*refs):
    *pieces, order, gate, up, sent, kept = refs
    rows = jnp.concatenate([piece[...] for piece in pieces], axis=0)
    features = jnp.dot(order[...], rows, preferred_element_type=F32).astype(BF16)
    half = order.shape[0] // NC
    width = gate.shape[1]
    for number, weight in ((0, gate), (1, up)):
        for col in range(0, width, 2 * BLOCK):
            product = jnp.dot(
                features, weight[:, col : col + 2 * BLOCK], preferred_element_type=F32
            )
            out = slice(number * width + col, number * width + col + 2 * BLOCK)
            kept[:, out] = product[:half]
            sent[:, out] = product[half:].astype(BF16)


def first_products(order, pieces, gate, up):
    count = sum(p.shape[0] for p in pieces)
    depth, width = gate.shape
    shape = (count // NC, 2 * width)
    return local_call(
        first_kernel,
        [(shape, BF16), (shape, F32)],
        *pieces,
        order,
        gate,
        up,
        flops=4 * count * depth * width,
    )


def columns(ref):
    return [slice(i, i + 2 * BLOCK) for i in range(0, ref.shape[1], 2 * BLOCK)]


def summed(kept, received, part, cols):
    step = kept.shape[0] // 8
    rows = slice(part * step, (part + 1) * step)
    return kept[rows, cols] + received[rows, cols].astype(F32)


def leave_kernel(kept, received, far0, far1, next1, back0):
    for part, out in ((4, far0), (5, far1), (3, next1), (6, back0)):
        for cols in columns(kept):
            out[:, cols] = summed(kept, received, part, cols).astype(BF16)


def relay_kernel(kept, received, relay0, relay1, through0, through1):
    for part, relay, out in ((2, relay0, through0), (7, relay1, through1)):
        for cols in columns(kept):
            value = summed(kept, received, part, cols) + relay[:, cols].astype(F32)
            out[:, cols] = value.astype(BF16)


def over_y_kernel(kept, received, direct0, direct1, through0, through1, mine, one, two, three):
    for part, direct, through in ((0, direct0, through0), (1, direct1, through1)):
        for cols in columns(kept):
            value = summed(kept, received, part, cols)
            value = value + direct[:, cols].astype(F32) + through[:, cols].astype(F32)
            for i in (0, 1):
                out = (mine, one, two, three)[2 * part + i]
                out[:, cols] = value[i * ROWS : (i + 1) * ROWS].astype(out.dtype)


def hidden_kernel(mine, one, two, three, hidden):
    width = hidden.shape[1]
    for cols in columns(hidden):
        gate, up = (
            mine[:, at]
            + one[:, at].astype(F32)
            + two[:, at].astype(F32)
            + three[:, at].astype(F32)
            for at in (cols, slice(width + cols.start, width + cols.stop))
        )
        hidden[:, cols] = (jax.nn.silu(gate) * up).astype(BF16)


def rows_kernel(a, b, c, d, out):
    for i, pair in ((0, (a, b)), (2, (c, d))):
        for cols in columns(out):
            value = jnp.concatenate([piece[:, cols].astype(F32) for piece in pair], axis=0)
            out[i * ROWS : (i + 2) * ROWS, cols] = value.astype(BF16)


def last_kernel(where, *refs):
    *hidden, weight, kept, one, two, three, terms = refs
    count = terms.shape[0]
    rows = jnp.concatenate([piece[...] for piece in hidden], axis=0)
    product = jnp.dot(rows, weight[...], preferred_element_type=F32)
    for place in range(count // ROWS):
        terms[pl.ds(turned_row(place, where), ROWS), :] = product[
            place * ROWS : (place + 1) * ROWS
        ]
    for i, out in enumerate((kept, one, two, three)):
        rows = slice(i * count // NX, (i + 1) * count // NX)
        out[...] = terms[rows, :].astype(out.dtype)


def last_products(where, pieces, weight):
    count = sum(p.shape[0] for p in pieces)
    depth, cols = weight.shape
    shape = (count // NX, cols)
    return local_call(
        last_kernel,
        [(shape, F32)] + [(shape, BF16)] * 3,
        *pieces,
        weight,
        scalars=[where],
        scratch=[pltpu.VMEM((count, cols), F32)],
        limit=12,
        flops=2 * count * depth * cols,
    )


def over_x_kernel(total, one, two, three, kept, sent):
    half = total.shape[0] // NL
    for i, out in ((1, sent), (0, kept)):
        rows = slice(i * half, (i + 1) * half)
        value = total[rows, :] + one[rows, :].astype(F32)
        value = value + two[rows, :].astype(F32) + three[rows, :].astype(F32)
        out[...] = value.astype(out.dtype)


def local(tokens, gate_payload, gate_scales, up_payload, up_scales, down_payload, down_scales):
    index = lax.axis_index("gx")
    where = jnp.stack([index % NC, (index // NC) % NY, index // (NY * NC)]).astype(jnp.int32)

    count = tokens.shape[0] * NL * NX
    (order,) = local_call(order_kernel, [((count, count), BF16)], scalars=[where])
    gate = weights(gate_payload, gate_scales, 4)
    up = weights(up_payload, up_scales, 4)
    pair = after(join(tokens, move_gy(tokens, dl=1)), gate, order)
    two, one, three = move_gy(pair, dx=2), move_gy(pair, dx=1), move_gy(pair, dx=3)
    pieces = [pair, one, two, after(three, up)]

    sent, kept = first_products(order, pieces, gate, up)
    received = move_gx(sent, dc=1)

    rows, cols = kept.shape
    step = (rows // 8, cols)
    far0, far1, next1, back0 = local_call(leave_kernel, [(step, BF16)] * 4, kept, received)
    relay0, relay1 = move_gx(far0, dy=1), move_gx(far1, dy=-1)
    direct1, direct0 = move_gx(next1, dy=1), move_gx(back0, dy=-1)
    through0, through1 = local_call(
        relay_kernel, [(step, BF16)] * 2, kept, received, relay0, relay1
    )
    down = weights(after(down_payload, through0), down_scales, 13)
    through0, through1 = move_gx(through0, dy=1), move_gx(through1, dy=-1)
    mine, one, two, three = local_call(
        over_y_kernel,
        [((ROWS, cols), F32)] + [((ROWS, cols), BF16)] * 3,
        after(kept, down),
        received,
        direct0,
        direct1,
        through0,
        through1,
    )
    two, one, three = move_gx(two, dz=2), move_gx(one, dz=1), move_gx(three, dz=3)
    units = cols // 2
    (hidden,) = local_call(hidden_kernel, [((ROWS, units), BF16)], mine, one, two, three)

    two, one, three = move_gx(hidden, dz=-2), move_gx(hidden, dz=-1), move_gx(hidden, dz=-3)
    (hidden,) = local_call(rows_kernel, [((NZ * ROWS, units), BF16)], hidden, one, two, three)
    two, one, three = move_gx(hidden, dy=-2), move_gx(hidden, dy=-1), move_gx(hidden, dy=-3)
    mine = [hidden, one, two, three]
    theirs = [move_gx(block, dc=1) for block in mine]
    total, one, two, three = last_products(where, mine + theirs, down)

    two, one, three = move_gy(two, dx=-2), move_gy(one, dx=-1), move_gy(three, dx=-3)
    shape = (total.shape[0] // NL, total.shape[1])
    total, sent = local_call(over_x_kernel, [(shape, F32), (shape, BF16)], total, one, two, three)
    return (total + move_gy(sent, dl=1).astype(F32)).astype(BF16)


def solution(mesh):
    placed = (
        P("gy", "gx"),
        P("gx", "gy"),
        P("gx", "gy"),
        P("gx", "gy"),
        P("gx", "gy"),
        P("gy", "gx"),
        P("gy", "gx"),
    )
    return jax.shard_map(
        local, mesh=mesh, in_specs=placed, out_specs=P("gy", "gx"), check_vma=False
    )
```

```python
import jax
import jax.numpy as jnp
from jax import lax
from jax.experimental import pallas as pl
from jax.experimental.pallas import tpu as pltpu
from jax.sharding import PartitionSpec as P

BLOCK = 128
F32 = jnp.float32
BF16 = jnp.bfloat16
NZ, NY, NC, NL, NX = 4, 4, 2, 2, 4
ROWS = 8
SMEM = pl.BlockSpec(memory_space=pltpu.SMEM)
VMEM = pl.BlockSpec(memory_space=pltpu.VMEM)
HBM = pl.BlockSpec(memory_space=pltpu.HBM)
MIB = 2**20


def move_gx(x, dz=0, dy=0, dc=0):
    pairs = []
    for z in range(NZ):
        for y in range(NY):
            for c in range(NC):
                src = (z * NY + y) * NC + c
                dst = (((z + dz) % NZ) * NY + (y + dy) % NY) * NC + (c + dc) % NC
                pairs.append((src, dst))
    return lax.ppermute(x, "gx", pairs)


def move_gy(x, dl=0, dx=0):
    pairs = []
    for l in range(NL):
        for i in range(NX):
            pairs.append((l * NX + i, (l + dl) % NL * NX + (i + dx) % NX))
    return lax.ppermute(x, "gy", pairs)


def after(x, *others):
    return lax.optimization_barrier((x, *others))[0]


def in_vmem(x):
    return pltpu.with_memory_space_constraint(x, pltpu.VMEM)


def local_call(kernel, outs, *arrays, scalars=(), scratch=(), limit=2, flops=0):
    moved = sum(a.size * a.dtype.itemsize for a in arrays)
    return pl.pallas_call(
        kernel,
        in_specs=[SMEM] * len(scalars) + [VMEM] * len(arrays),
        out_specs=[VMEM] * len(outs),
        out_shape=[pltpu.VMEM(shape, dtype) for shape, dtype in outs],
        scratch_shapes=list(scratch),
        compiler_params=pltpu.CompilerParams(vmem_limit_bytes=limit * MIB),
        cost_estimate=pl.CostEstimate(flops=flops, bytes_accessed=moved, transcendentals=0),
    )(*scalars, *[in_vmem(a) for a in arrays])


def weights_kernel(steps, flipped, payload, scales, out, held, factors, sems, sem):
    rows = payload.shape[0] // steps
    copies = [
        pltpu.make_async_copy(
            payload.at[pl.ds(i * rows, rows)], held.at[pl.ds(i * rows, rows)], sems.at[i]
        )
        for i in range(steps)
    ]
    small = pltpu.make_async_copy(scales, factors, sem)
    small.start()
    for copy in copies:
        copy.start()
    small.wait()
    for i, copy in enumerate(copies):
        copy.wait()
        for row in range(i * rows // BLOCK, (i + 1) * rows // BLOCK):
            for col in range(payload.shape[1] // BLOCK):
                at = (
                    slice(row * BLOCK, (row + 1) * BLOCK),
                    slice(col * BLOCK, (col + 1) * BLOCK),
                )
                factor = factors[col, row] if flipped else factors[row, col]
                out[at] = (held[at].astype(F32) * factor).astype(BF16)


def in_hbm(x):
    return pltpu.with_memory_space_constraint(x, pltpu.HBM)


def weights(payload, scales, steps, flipped=False):
    rows, cols = payload.shape
    return pl.pallas_call(
        lambda *refs: weights_kernel(steps, flipped, *refs),
        in_specs=[HBM, HBM],
        out_specs=VMEM,
        out_shape=pltpu.VMEM((rows, cols), BF16),
        scratch_shapes=[
            pltpu.VMEM((rows, cols), BF16),
            pltpu.SMEM(scales.shape, F32),
            pltpu.SemaphoreType.DMA((steps,)),
            pltpu.SemaphoreType.DMA,
        ],
        compiler_params=pltpu.CompilerParams(vmem_limit_bytes=5 * MIB),
        cost_estimate=pl.CostEstimate(
            flops=rows * cols, bytes_accessed=4 * rows * cols, transcendentals=0
        ),
    )(in_hbm(payload), in_hbm(scales))


def join_kernel(*refs):
    *pieces, out = refs
    at = 0
    for piece in pieces:
        rows = piece.shape[0]
        out[at : at + rows, :] = piece[...]
        at += rows


def join(*pieces):
    shape = (sum(p.shape[0] for p in pieces), pieces[0].shape[1])
    return local_call(join_kernel, [(shape, BF16)], *pieces)[0]


def order_kernel(where, out):
    row = lax.broadcasted_iota(jnp.int32, out.shape, 0)
    column = lax.broadcasted_iota(jnp.int32, out.shape, 1)
    block, inner = row // ROWS, row % ROWS
    c, y, z = block // (NY * NZ), block // NZ % NY, block % NZ
    c, y, z = (where[0] + c) % NC, (where[1] + y) % NY, (where[2] + z) % NZ
    chosen = ((c * NY + y) * NZ + z) * ROWS + inner
    out[...] = jnp.where(chosen == column, 1.0, 0.0).astype(BF16)


def turned_row(place, where):
    c, y, z = place // (NY * NZ), place // NZ % NY, place % NZ
    c, y, z = (where[0] + c) % NC, (where[1] + y) % NY, (where[2] + z) % NZ
    return pl.multiple_of(((c * NY + y) * NZ + z) * ROWS, ROWS)


def products(features, gate, up):
    width = gate.shape[1]
    for number, weight in ((0, gate), (1, up)):
        for col in range(0, width, 2 * BLOCK):
            out = slice(number * width + col, number * width + col + 2 * BLOCK)
            yield out, jnp.dot(
                features, weight[:, col : col + 2 * BLOCK], preferred_element_type=F32
            )


def sent_kernel(*refs):
    *pieces, order, gate, up, mine, sent = refs
    rows = jnp.concatenate([piece[...] for piece in pieces], axis=0)
    features = jnp.dot(order[...], rows, preferred_element_type=F32).astype(BF16)
    half = order.shape[0] // NC
    mine[...] = features[:half]
    for out, product in products(features[half:], gate, up):
        sent[:, out] = product.astype(BF16)


def kept_kernel(features, gate, up, kept):
    for out, product in products(features[...], gate, up):
        kept[:, out] = product


def columns(width, step):
    return [slice(i, i + step) for i in range(0, width, step)]


def over_columns(width, step, body):
    @pl.loop(0, width // step)
    def _(i):
        body(pl.multiple_of(i * step, step))


def summed(kept, received, part, cols):
    step = kept.shape[0] // 8
    rows = slice(part * step, (part + 1) * step)
    return kept[rows, cols] + received[rows, cols].astype(F32)


def leave_kernel(kept, received, far0, far1, next1, back0):
    def body(at):
        cols = pl.ds(at, 13 * BLOCK)
        for part, out in ((4, far0), (5, far1), (3, next1), (6, back0)):
            out[:, cols] = summed(kept, received, part, cols).astype(BF16)

    over_columns(kept.shape[1], 13 * BLOCK, body)


def relay_kernel(kept, received, relay0, relay1, through0, through1):
    def body(at):
        cols = pl.ds(at, 13 * BLOCK)
        for part, relay, out in ((2, relay0, through0), (7, relay1, through1)):
            value = summed(kept, received, part, cols) + relay[:, cols].astype(F32)
            out[:, cols] = value.astype(BF16)

    over_columns(kept.shape[1], 13 * BLOCK, body)


def over_y_kernel(part, kept, received, direct, through, first, second):
    width = kept.shape[1] // 2

    def body(at):
        values = []
        for place in (0, width):
            cols = pl.ds(pl.multiple_of(place + at, BLOCK), 13 * BLOCK)
            value = summed(kept, received, part, cols)
            values.append(value + direct[:, cols].astype(F32) + through[:, cols].astype(F32))
        for i, out in enumerate((first, second)):
            both = jnp.concatenate([v[i * ROWS : (i + 1) * ROWS] for v in values], axis=0)
            out[:, pl.ds(at, 13 * BLOCK)] = both.astype(out.dtype)

    over_columns(width, 13 * BLOCK, body)


def hidden_kernel(mine, one, two, three, hidden):
    for cols in columns(hidden.shape[1], 2 * BLOCK):
        total = mine[:, cols] + one[:, cols].astype(F32)
        total = total + two[:, cols].astype(F32) + three[:, cols].astype(F32)
        hidden[:, cols] = (jax.nn.silu(total[:ROWS]) * total[ROWS:]).astype(BF16)


def rows_kernel(a, b, c, d, out):
    for i, pair in ((0, (a, b)), (2, (c, d))):
        for cols in columns(out.shape[1], 2 * BLOCK):
            value = jnp.concatenate([piece[:, cols].astype(F32) for piece in pair], axis=0)
            out[i * ROWS : (i + 2) * ROWS, cols] = value.astype(BF16)


def mine_kernel(*refs):
    *hidden, weight, out = refs
    rows = jnp.concatenate([piece[...] for piece in hidden], axis=0)
    out[...] = jnp.dot(rows, weight[...], preferred_element_type=F32)


def last_kernel(where, mine, *refs):
    *hidden, weight, kept, one, two, three, terms = refs
    half = mine.shape[0]
    rows = jnp.concatenate([piece[...] for piece in hidden], axis=0)
    for place in range(half // ROWS):
        terms[pl.ds(turned_row(place, where), ROWS), :] = mine[place * ROWS : (place + 1) * ROWS, :]
    product = jnp.dot(rows, weight[...], preferred_element_type=F32)
    for place in range(half // ROWS):
        terms[pl.ds(turned_row(half // ROWS + place, where), ROWS), :] = product[
            place * ROWS : (place + 1) * ROWS
        ]
    for i, out in enumerate((kept, one, two, three)):
        rows = slice(i * 2 * half // NX, (i + 1) * 2 * half // NX)
        out[...] = terms[rows, :].astype(out.dtype)


def last_products(where, mine, theirs, weight):
    half = sum(p.shape[0] for p in mine)
    depth, cols = weight.shape
    flops = 2 * half * depth * cols
    (product,) = local_call(mine_kernel, [((half, cols), F32)], *mine, weight, flops=flops)
    shape = (2 * half // NX, cols)
    return local_call(
        last_kernel,
        [(shape, F32)] + [(shape, BF16)] * 3,
        product,
        *theirs,
        weight,
        scalars=[where],
        scratch=[pltpu.VMEM((2 * half, cols), F32)],
        limit=4,
        flops=flops,
    )


def over_x_kernel(total, one, two, three, kept, sent):
    half = total.shape[0] // NL
    for i, out in ((1, sent), (0, kept)):
        rows = slice(i * half, (i + 1) * half)
        value = total[rows, :] + one[rows, :].astype(F32)
        value = value + two[rows, :].astype(F32) + three[rows, :].astype(F32)
        out[...] = value.astype(out.dtype)


def local(tokens, gate_payload, gate_scales, up_payload, up_scales, down_payload, down_scales):
    index = lax.axis_index("gx")
    where = jnp.stack([index % NC, (index // NC) % NY, index // (NY * NC)]).astype(jnp.int32)

    count = tokens.shape[0] * NL * NX
    gate = weights(gate_payload, gate_scales, 4)
    (order,) = local_call(order_kernel, [((count, count), BF16)], scalars=[where])
    pair = after(join(tokens, move_gy(tokens, dl=1)), gate, order)
    up = weights(after(up_payload, pair), up_scales, 4)
    two, one, three = move_gy(pair, dx=2), move_gy(pair, dx=1), move_gy(pair, dx=3)
    pieces = [pair, one, two, after(three, up)]

    depth, cols = gate.shape[0], 2 * gate.shape[1]
    rows = count // NC
    flops = 2 * rows * depth * cols
    features, sent = local_call(
        sent_kernel,
        [((rows, depth), BF16), ((rows, cols), BF16)],
        *pieces,
        order,
        gate,
        up,
        flops=flops,
    )
    received = move_gx(sent, dc=1)
    (kept,) = local_call(kept_kernel, [((rows, cols), F32)], features, gate, up, flops=flops)

    step = (rows // 8, cols)
    far0, far1, next1, back0 = local_call(leave_kernel, [(step, BF16)] * 4, kept, received)
    relay0, relay1 = move_gx(far0, dy=1), move_gx(far1, dy=-1)
    direct1, direct0 = move_gx(next1, dy=1), move_gx(back0, dy=-1)
    through0, through1 = local_call(
        relay_kernel, [(step, BF16)] * 2, kept, received, relay0, relay1
    )
    down = weights(after(down_payload, through0), down_scales.T, 13, flipped=True)
    through0, through1 = move_gx(through0, dy=1), move_gx(through1, dy=-1)
    units = cols // 2
    piece = (2 * ROWS, units)
    kept = after(kept, down)
    two, three = local_call(
        lambda *refs: over_y_kernel(1, *refs),
        [(piece, BF16)] * 2,
        kept,
        received,
        direct1,
        through1,
    )
    two = move_gx(two, dz=2)
    mine, one = local_call(
        lambda *refs: over_y_kernel(0, *refs),
        [(piece, F32), (piece, BF16)],
        kept,
        received,
        direct0,
        through0,
    )
    one, three = move_gx(one, dz=1), move_gx(three, dz=3)
    (hidden,) = local_call(hidden_kernel, [((ROWS, units), BF16)], mine, one, two, three)

    two, one, three = move_gx(hidden, dz=-2), move_gx(hidden, dz=-1), move_gx(hidden, dz=-3)
    (hidden,) = local_call(rows_kernel, [((NZ * ROWS, units), BF16)], hidden, one, two, three)
    two, one, three = move_gx(hidden, dy=-2), move_gx(hidden, dy=-1), move_gx(hidden, dy=-3)
    mine = [hidden, one, two, three]
    theirs = [move_gx(hidden, dc=1)]
    theirs += [move_gx(after(block, one, two, three), dc=1) for block in mine[1:]]
    total, one, two, three = last_products(where, mine, theirs, down)

    two, one, three = move_gy(two, dx=-2), move_gy(one, dx=-1), move_gy(three, dx=-3)
    shape = (total.shape[0] // NL, total.shape[1])
    total, sent = local_call(over_x_kernel, [(shape, F32), (shape, BF16)], total, one, two, three)
    return (total + move_gy(sent, dl=1).astype(F32)).astype(BF16)


def solution(mesh):
    placed = (
        P("gy", "gx"),
        P("gx", "gy"),
        P("gx", "gy"),
        P("gx", "gy"),
        P("gx", "gy"),
        P("gy", "gx"),
        P("gy", "gx"),
    )
    return jax.shard_map(
        local, mesh=mesh, in_specs=placed, out_specs=P("gy", "gx"), check_vma=False
    )
```

```python
import jax
import jax.numpy as jnp
from jax import lax
from jax.experimental import pallas as pl
from jax.experimental.pallas import tpu as pltpu
from jax.sharding import PartitionSpec as P

BLOCK = 128
F32 = jnp.float32
BF16 = jnp.bfloat16
NZ, NY, NC, NL, NX = 4, 4, 2, 2, 4
ROWS = 8
VMEM = pl.BlockSpec(memory_space=pltpu.VMEM)
HBM = pl.BlockSpec(memory_space=pltpu.HBM)
MIB = 2**20


def move_gx(x, dz=0, dy=0, dc=0):
    pairs = []
    for z in range(NZ):
        for y in range(NY):
            for c in range(NC):
                src = (z * NY + y) * NC + c
                dst = (((z + dz) % NZ) * NY + (y + dy) % NY) * NC + (c + dc) % NC
                pairs.append((src, dst))
    return lax.ppermute(x, "gx", pairs)


def move_gy(x, dl=0, dx=0):
    pairs = []
    for l in range(NL):
        for i in range(NX):
            pairs.append((l * NX + i, (l + dl) % NL * NX + (i + dx) % NX))
    return lax.ppermute(x, "gy", pairs)


def after(x, *others):
    return lax.optimization_barrier((x, *others))[0]


def in_vmem(x):
    return pltpu.with_memory_space_constraint(x, pltpu.VMEM)


def local_call(kernel, outs, *arrays, scratch=(), limit=2, flops=0):
    moved = sum(a.size * a.dtype.itemsize for a in arrays)
    return pl.pallas_call(
        kernel,
        in_specs=[VMEM] * len(arrays),
        out_specs=[VMEM] * len(outs),
        out_shape=[pltpu.VMEM(shape, dtype) for shape, dtype in outs],
        scratch_shapes=list(scratch),
        compiler_params=pltpu.CompilerParams(vmem_limit_bytes=limit * MIB),
        cost_estimate=pl.CostEstimate(flops=flops, bytes_accessed=moved, transcendentals=0),
    )(*[in_vmem(a) for a in arrays])


def weights_kernel(steps, flipped, payload, scales, out, held, factors, sems, sem):
    rows = payload.shape[0] // steps
    copies = [
        pltpu.make_async_copy(
            payload.at[pl.ds(i * rows, rows)], held.at[pl.ds(i * rows, rows)], sems.at[i]
        )
        for i in range(steps)
    ]
    small = pltpu.make_async_copy(scales, factors, sem)
    small.start()
    for copy in copies:
        copy.start()
    small.wait()
    for i, copy in enumerate(copies):
        copy.wait()
        for row in range(i * rows // BLOCK, (i + 1) * rows // BLOCK):
            for col in range(payload.shape[1] // BLOCK):
                at = (
                    slice(row * BLOCK, (row + 1) * BLOCK),
                    slice(col * BLOCK, (col + 1) * BLOCK),
                )
                factor = factors[col, row] if flipped else factors[row, col]
                out[at] = (held[at].astype(F32) * factor).astype(BF16)


def in_hbm(x):
    return pltpu.with_memory_space_constraint(x, pltpu.HBM)


def weights(payload, scales, steps, flipped=False):
    rows, cols = payload.shape
    return pl.pallas_call(
        lambda *refs: weights_kernel(steps, flipped, *refs),
        in_specs=[HBM, HBM],
        out_specs=VMEM,
        out_shape=pltpu.VMEM((rows, cols), BF16),
        scratch_shapes=[
            pltpu.VMEM((rows, cols), BF16),
            pltpu.SMEM(scales.shape, F32),
            pltpu.SemaphoreType.DMA((steps,)),
            pltpu.SemaphoreType.DMA,
        ],
        compiler_params=pltpu.CompilerParams(vmem_limit_bytes=5 * MIB),
        cost_estimate=pl.CostEstimate(
            flops=rows * cols, bytes_accessed=4 * rows * cols, transcendentals=0
        ),
    )(in_hbm(payload), in_hbm(scales))


def join_kernel(*refs):
    *pieces, out = refs
    at = 0
    for piece in pieces:
        rows = piece.shape[0]
        out[at : at + rows, :] = piece[...]
        at += rows


def join(*pieces):
    shape = (sum(p.shape[0] for p in pieces), pieces[0].shape[1])
    return local_call(join_kernel, [(shape, BF16)], *pieces)[0]


def position():
    index = lax.axis_index("gx")
    return index % NC, index // NC % NY, index // (NY * NC)


def order_kernel(out):
    where = position()
    step = 2 * ROWS
    for at in range(0, out.shape[0], step):
        row = lax.broadcasted_iota(jnp.int32, (step, out.shape[1]), 0)
        column = lax.broadcasted_iota(jnp.int32, (step, out.shape[1]), 1)
        first, second = (turned_row(at // ROWS + i, where) for i in (0, 1))
        chosen = jnp.where(row < ROWS, first, second - ROWS) + row
        out[at : at + step, :] = jnp.where(chosen == column, 1.0, 0.0).astype(BF16)


def turned_row(place, where):
    c, y, z = place // (NY * NZ), place // NZ % NY, place % NZ
    c, y, z = (where[0] + c) % NC, (where[1] + y) % NY, (where[2] + z) % NZ
    return pl.multiple_of(((c * NY + y) * NZ + z) * ROWS, ROWS)


def products(features, gate, up):
    width = gate.shape[1]
    for number, weight in ((0, gate), (1, up)):
        for col in range(0, width, 2 * BLOCK):
            out = slice(number * width + col, number * width + col + 2 * BLOCK)
            yield out, jnp.dot(
                features, weight[:, col : col + 2 * BLOCK], preferred_element_type=F32
            )


def sent_kernel(*refs):
    *pieces, order, gate, up, mine, sent = refs
    rows = jnp.concatenate([piece[...] for piece in pieces], axis=0)
    features = jnp.dot(order[...], rows, preferred_element_type=F32).astype(BF16)
    half = order.shape[0] // NC
    mine[...] = features[:half]
    for out, product in products(features[half:], gate, up):
        sent[:, out] = product.astype(BF16)


def kept_kernel(features, gate, up, kept):
    for out, product in products(features[...], gate, up):
        kept[:, out] = product


def columns(width, step):
    return [slice(i, i + step) for i in range(0, width, step)]


def over_columns(width, step, body):
    @pl.loop(0, width // step)
    def _(i):
        body(pl.multiple_of(i * step, step))


def summed(kept, received, part, cols):
    step = kept.shape[0] // 8
    rows = slice(part * step, (part + 1) * step)
    return kept[rows, cols] + received[rows, cols].astype(F32)


def leave_kernel(kept, received, far0, far1, next1, back0):
    def body(at):
        cols = pl.ds(at, 13 * BLOCK)
        for part, out in ((4, far0), (5, far1), (3, next1), (6, back0)):
            out[:, cols] = summed(kept, received, part, cols).astype(BF16)

    over_columns(kept.shape[1], 13 * BLOCK, body)


def relay_kernel(part, kept, received, relay, through):
    def body(at):
        cols = pl.ds(at, 13 * BLOCK)
        value = summed(kept, received, part, cols) + relay[:, cols].astype(F32)
        through[:, cols] = value.astype(BF16)

    over_columns(kept.shape[1], 13 * BLOCK, body)


def over_y_kernel(part, kept, received, direct, through, first, second):
    width = kept.shape[1] // 2

    def body(at):
        values = []
        for place in (0, width):
            cols = pl.ds(pl.multiple_of(place + at, BLOCK), 13 * BLOCK)
            value = summed(kept, received, part, cols)
            values.append(value + direct[:, cols].astype(F32) + through[:, cols].astype(F32))
        for i, out in enumerate((first, second)):
            both = jnp.concatenate([v[i * ROWS : (i + 1) * ROWS] for v in values], axis=0)
            out[:, pl.ds(at, 13 * BLOCK)] = both.astype(out.dtype)

    over_columns(width, 13 * BLOCK, body)


def hidden_kernel(mine, one, two, three, hidden):
    for cols in columns(hidden.shape[1], 2 * BLOCK):
        total = mine[:, cols] + one[:, cols].astype(F32)
        total = total + two[:, cols].astype(F32) + three[:, cols].astype(F32)
        hidden[:, cols] = (jax.nn.silu(total[:ROWS]) * total[ROWS:]).astype(BF16)


def rows_kernel(a, b, c, d, out):
    for i, pair in ((0, (a, b)), (2, (c, d))):
        for cols in columns(out.shape[1], 2 * BLOCK):
            value = jnp.concatenate([piece[:, cols].astype(F32) for piece in pair], axis=0)
            out[i * ROWS : (i + 2) * ROWS, cols] = value.astype(BF16)


def mine_kernel(*refs):
    *hidden, weight, out = refs
    rows = jnp.concatenate([piece[...] for piece in hidden], axis=0)
    out[...] = jnp.dot(rows, weight[...], preferred_element_type=F32)


def last_kernel(mine, *refs):
    where = position()
    *hidden, weight, kept, one, two, three, terms = refs
    half = mine.shape[0]
    rows = jnp.concatenate([piece[...] for piece in hidden], axis=0)
    for place in range(half // ROWS):
        terms[pl.ds(turned_row(place, where), ROWS), :] = mine[place * ROWS : (place + 1) * ROWS, :]
    product = jnp.dot(rows, weight[...], preferred_element_type=F32)
    for place in range(half // ROWS):
        terms[pl.ds(turned_row(half // ROWS + place, where), ROWS), :] = product[
            place * ROWS : (place + 1) * ROWS
        ]
    for i, out in enumerate((kept, one, two, three)):
        rows = slice(i * 2 * half // NX, (i + 1) * 2 * half // NX)
        out[...] = terms[rows, :].astype(out.dtype)


def last_products(mine, theirs, weight):
    half = sum(p.shape[0] for p in mine)
    depth, cols = weight.shape
    flops = 2 * half * depth * cols
    (product,) = local_call(mine_kernel, [((half, cols), F32)], *mine, weight, flops=flops)
    shape = (2 * half // NX, cols)
    return local_call(
        last_kernel,
        [(shape, F32)] + [(shape, BF16)] * 3,
        product,
        *theirs,
        weight,
        scratch=[pltpu.VMEM((2 * half, cols), F32)],
        limit=4,
        flops=flops,
    )


def over_x_kernel(total, one, two, three, kept, sent):
    half = total.shape[0] // NL
    for i, out in ((1, sent), (0, kept)):
        rows = slice(i * half, (i + 1) * half)
        value = total[rows, :] + one[rows, :].astype(F32)
        value = value + two[rows, :].astype(F32) + three[rows, :].astype(F32)
        out[...] = value.astype(out.dtype)


def local(tokens, gate_payload, gate_scales, up_payload, up_scales, down_payload, down_scales):
    count = tokens.shape[0] * NL * NX
    gate = weights(gate_payload, gate_scales, 4)
    (order,) = local_call(order_kernel, [((count, count), BF16)])
    pair = after(join(tokens, move_gy(tokens, dl=1)), gate, order)
    up = weights(after(up_payload, pair), up_scales, 4)
    two, one, three = move_gy(pair, dx=2), move_gy(pair, dx=1), move_gy(pair, dx=3)
    pieces = [pair, one, two, after(three, up)]

    depth, cols = gate.shape[0], 2 * gate.shape[1]
    rows = count // NC
    flops = 2 * rows * depth * cols
    features, sent = local_call(
        sent_kernel,
        [((rows, depth), BF16), ((rows, cols), BF16)],
        *pieces,
        order,
        gate,
        up,
        flops=flops,
    )
    received = move_gx(sent, dc=1)
    (kept,) = local_call(kept_kernel, [((rows, cols), F32)], features, gate, up, flops=flops)

    step = (rows // 8, cols)
    far0, far1, next1, back0 = local_call(leave_kernel, [(step, BF16)] * 4, kept, received)
    relay0, relay1 = move_gx(far0, dy=1), move_gx(far1, dy=-1)
    direct1, direct0 = move_gx(next1, dy=1), move_gx(back0, dy=-1)
    (through1,) = local_call(
        lambda *refs: relay_kernel(7, *refs), [(step, BF16)], kept, received, relay1
    )
    (through0,) = local_call(
        lambda *refs: relay_kernel(2, *refs), [(step, BF16)], kept, received, after(relay0, through1)
    )
    down = weights(after(down_payload, through0), down_scales.T, 13, flipped=True)
    through1, through0 = move_gx(through1, dy=-1), move_gx(through0, dy=1)
    units = cols // 2
    piece = (2 * ROWS, units)
    kept = after(kept, down)
    two, three = local_call(
        lambda *refs: over_y_kernel(1, *refs),
        [(piece, BF16)] * 2,
        kept,
        received,
        direct1,
        through1,
    )
    two = move_gx(two, dz=2)
    mine, one = local_call(
        lambda *refs: over_y_kernel(0, *refs),
        [(piece, F32), (piece, BF16)],
        kept,
        received,
        direct0,
        through0,
    )
    one, three = move_gx(one, dz=1), move_gx(three, dz=3)
    (hidden,) = local_call(hidden_kernel, [((ROWS, units), BF16)], mine, one, two, three)

    two, one, three = move_gx(hidden, dz=-2), move_gx(hidden, dz=-1), move_gx(hidden, dz=-3)
    (hidden,) = local_call(rows_kernel, [((NZ * ROWS, units), BF16)], hidden, one, two, three)
    two, one, three = move_gx(hidden, dy=-2), move_gx(hidden, dy=-1), move_gx(hidden, dy=-3)
    mine = [hidden, one, two, three]
    theirs = [move_gx(hidden, dc=1)]
    theirs += [move_gx(block, dc=1) for block in mine[1:]]
    total, one, two, three = last_products(mine, theirs, down)

    two, one, three = move_gy(two, dx=-2), move_gy(one, dx=-1), move_gy(three, dx=-3)
    shape = (total.shape[0] // NL, total.shape[1])
    total, sent = local_call(over_x_kernel, [(shape, F32), (shape, BF16)], total, one, two, three)
    return (total + move_gy(sent, dl=1).astype(F32)).astype(BF16)


def solution(mesh):
    placed = (
        P("gy", "gx"),
        P("gx", "gy"),
        P("gx", "gy"),
        P("gx", "gy"),
        P("gx", "gy"),
        P("gy", "gx"),
        P("gy", "gx"),
    )
    return jax.shard_map(
        local, mesh=mesh, in_specs=placed, out_specs=P("gy", "gx"), check_vma=False
    )
```

```python
import jax
import jax.numpy as jnp
from jax import lax
from jax.experimental import pallas as pl
from jax.experimental.pallas import tpu as pltpu
from jax.sharding import PartitionSpec as P

BLOCK = 128
F32 = jnp.float32
BF16 = jnp.bfloat16
NZ, NY, NC, NL, NX = 4, 4, 2, 2, 4
ROWS = 8
VMEM = pl.BlockSpec(memory_space=pltpu.VMEM)
HBM = pl.BlockSpec(memory_space=pltpu.HBM)
MIB = 2**20


def move_gx(x, dz=0, dy=0, dc=0):
    pairs = []
    for z in range(NZ):
        for y in range(NY):
            for c in range(NC):
                src = (z * NY + y) * NC + c
                dst = (((z + dz) % NZ) * NY + (y + dy) % NY) * NC + (c + dc) % NC
                pairs.append((src, dst))
    return lax.ppermute(x, "gx", pairs)


def move_gy(x, dl=0, dx=0):
    pairs = []
    for l in range(NL):
        for i in range(NX):
            pairs.append((l * NX + i, (l + dl) % NL * NX + (i + dx) % NX))
    return lax.ppermute(x, "gy", pairs)


def after(x, *others):
    return lax.optimization_barrier((x, *others))[0]


def in_vmem(x):
    return pltpu.with_memory_space_constraint(x, pltpu.VMEM)


def local_call(kernel, outs, *arrays, scratch=(), limit=2, flops=0):
    moved = sum(a.size * a.dtype.itemsize for a in arrays)
    return pl.pallas_call(
        kernel,
        in_specs=[VMEM] * len(arrays),
        out_specs=[VMEM] * len(outs),
        out_shape=[pltpu.VMEM(shape, dtype) for shape, dtype in outs],
        scratch_shapes=list(scratch),
        compiler_params=pltpu.CompilerParams(vmem_limit_bytes=limit * MIB),
        cost_estimate=pl.CostEstimate(flops=flops, bytes_accessed=moved, transcendentals=0),
    )(*[in_vmem(a) for a in arrays])


def weights_kernel(steps, flipped, payload, scales, out, held, factors, sems, sem):
    rows = payload.shape[0] // steps
    copies = [
        pltpu.make_async_copy(
            payload.at[pl.ds(i * rows, rows)], held.at[pl.ds(i * rows, rows)], sems.at[i]
        )
        for i in range(steps)
    ]
    small = pltpu.make_async_copy(scales, factors, sem)
    small.start()
    for copy in copies:
        copy.start()
    small.wait()
    for i, copy in enumerate(copies):
        copy.wait()
        for row in range(i * rows // BLOCK, (i + 1) * rows // BLOCK):
            for col in range(payload.shape[1] // BLOCK):
                at = (
                    slice(row * BLOCK, (row + 1) * BLOCK),
                    slice(col * BLOCK, (col + 1) * BLOCK),
                )
                factor = factors[col, row] if flipped else factors[row, col]
                out[at] = (held[at].astype(F32) * factor).astype(BF16)


def in_hbm(x):
    return pltpu.with_memory_space_constraint(x, pltpu.HBM)


def weights(payload, scales, steps, flipped=False):
    rows, cols = payload.shape
    return pl.pallas_call(
        lambda *refs: weights_kernel(steps, flipped, *refs),
        in_specs=[HBM, HBM],
        out_specs=VMEM,
        out_shape=pltpu.VMEM((rows, cols), BF16),
        scratch_shapes=[
            pltpu.VMEM((rows, cols), BF16),
            pltpu.SMEM(scales.shape, F32),
            pltpu.SemaphoreType.DMA((steps,)),
            pltpu.SemaphoreType.DMA,
        ],
        compiler_params=pltpu.CompilerParams(vmem_limit_bytes=5 * MIB),
        cost_estimate=pl.CostEstimate(
            flops=rows * cols, bytes_accessed=4 * rows * cols, transcendentals=0
        ),
    )(in_hbm(payload), in_hbm(scales))


def join_kernel(*refs):
    *pieces, out = refs
    at = 0
    for piece in pieces:
        rows = piece.shape[0]
        out[at : at + rows, :] = piece[...]
        at += rows


def join(*pieces):
    shape = (sum(p.shape[0] for p in pieces), pieces[0].shape[1])
    return local_call(join_kernel, [(shape, BF16)], *pieces)[0]


def position():
    index = lax.axis_index("gx")
    return index % NC, index // NC % NY, index // (NY * NC)


def order_kernel(out):
    where = position()
    step = 2 * ROWS
    for at in range(0, out.shape[0], step):
        row = lax.broadcasted_iota(jnp.int32, (step, out.shape[1]), 0)
        column = lax.broadcasted_iota(jnp.int32, (step, out.shape[1]), 1)
        first, second = (turned_row(at // ROWS + i, where) for i in (0, 1))
        chosen = jnp.where(row < ROWS, first, second - ROWS) + row
        out[at : at + step, :] = jnp.where(chosen == column, 1.0, 0.0).astype(BF16)


def turned_row(place, where):
    c, y, z = place // (NY * NZ), place // NZ % NY, place % NZ
    c, y, z = (where[0] + c) % NC, (where[1] + y) % NY, (where[2] + z) % NZ
    return pl.multiple_of(((c * NY + y) * NZ + z) * ROWS, ROWS)


def products(features, gate, up):
    width = gate.shape[1]
    for number, weight in ((0, gate), (1, up)):
        for col in range(0, width, 2 * BLOCK):
            out = slice(number * width + col, number * width + col + 2 * BLOCK)
            yield out, jnp.dot(
                features, weight[:, col : col + 2 * BLOCK], preferred_element_type=F32
            )


def sent_kernel(*refs):
    *pieces, order, gate, up, mine, sent = refs
    rows = jnp.concatenate([piece[...] for piece in pieces], axis=0)
    features = jnp.dot(order[...], rows, preferred_element_type=F32).astype(BF16)
    half = order.shape[0] // NC
    mine[...] = features[:half]
    for out, product in products(features[half:], gate, up):
        sent[:, out] = product.astype(BF16)


def kept_kernel(features, gate, up, kept):
    for out, product in products(features[...], gate, up):
        kept[:, out] = product


def columns(width, step):
    return [slice(i, i + step) for i in range(0, width, step)]


def over_columns(width, step, body):
    @pl.loop(0, width // step)
    def _(i):
        body(pl.multiple_of(i * step, step))


def summed(kept, received, part, cols):
    step = kept.shape[0] // 8
    rows = slice(part * step, (part + 1) * step)
    return kept[rows, cols] + received[rows, cols].astype(F32)


def leave_kernel(kept, received, far0, far1, next1, back0):
    def body(at):
        cols = pl.ds(at, 13 * BLOCK)
        for part, out in ((4, far0), (5, far1), (3, next1), (6, back0)):
            out[:, cols] = summed(kept, received, part, cols).astype(BF16)

    over_columns(kept.shape[1], 13 * BLOCK, body)


def relay_kernel(part, kept, received, relay, through):
    def body(at):
        cols = pl.ds(at, 13 * BLOCK)
        value = summed(kept, received, part, cols) + relay[:, cols].astype(F32)
        through[:, cols] = value.astype(BF16)

    over_columns(kept.shape[1], 13 * BLOCK, body)


def over_y_kernel(part, kept, received, direct, through, first, second):
    width = kept.shape[1] // 2

    def body(at):
        values = []
        for place in (0, width):
            cols = pl.ds(pl.multiple_of(place + at, BLOCK), 13 * BLOCK)
            value = summed(kept, received, part, cols)
            values.append(value + direct[:, cols].astype(F32) + through[:, cols].astype(F32))
        for i, out in enumerate((first, second)):
            both = jnp.concatenate([v[i * ROWS : (i + 1) * ROWS] for v in values], axis=0)
            out[:, pl.ds(at, 13 * BLOCK)] = both.astype(out.dtype)

    over_columns(width, 13 * BLOCK, body)


def hidden_kernel(mine, one, two, three, hidden):
    for cols in columns(hidden.shape[1], 2 * BLOCK):
        total = mine[:, cols] + one[:, cols].astype(F32)
        total = total + two[:, cols].astype(F32) + three[:, cols].astype(F32)
        hidden[:, cols] = (jax.nn.silu(total[:ROWS]) * total[ROWS:]).astype(BF16)


def corner_kernel(x, out):
    out[...] = x[: out.shape[0], : out.shape[1]]


def first_awaited(first, *others):
    (corner,) = local_call(corner_kernel, [((8, BLOCK), first.dtype)], first)
    return [after(x, corner) for x in others]


def rows_kernel(a, b, c, d, out):
    for i, pair in ((0, (a, b)), (2, (c, d))):
        for cols in columns(out.shape[1], 2 * BLOCK):
            value = jnp.concatenate([piece[:, cols].astype(F32) for piece in pair], axis=0)
            out[i * ROWS : (i + 2) * ROWS, cols] = value.astype(BF16)


def mine_kernel(*refs):
    *hidden, weight, out = refs
    rows = jnp.concatenate([piece[...] for piece in hidden], axis=0)
    out[...] = jnp.dot(rows, weight[...], preferred_element_type=F32)


def last_kernel(mine, *refs):
    where = position()
    *hidden, weight, kept, one, two, three, terms = refs
    half = mine.shape[0]
    rows = jnp.concatenate([piece[...] for piece in hidden], axis=0)
    for place in range(half // ROWS):
        terms[pl.ds(turned_row(place, where), ROWS), :] = mine[place * ROWS : (place + 1) * ROWS, :]
    product = jnp.dot(rows, weight[...], preferred_element_type=F32)
    for place in range(half // ROWS):
        terms[pl.ds(turned_row(half // ROWS + place, where), ROWS), :] = product[
            place * ROWS : (place + 1) * ROWS
        ]
    for i, out in enumerate((kept, one, two, three)):
        rows = slice(i * 2 * half // NX, (i + 1) * 2 * half // NX)
        out[...] = terms[rows, :].astype(out.dtype)


def last_products(mine, theirs, weight):
    half = sum(p.shape[0] for p in mine)
    depth, cols = weight.shape
    flops = 2 * half * depth * cols
    (product,) = local_call(mine_kernel, [((half, cols), F32)], *mine, weight, flops=flops)
    shape = (2 * half // NX, cols)
    return local_call(
        last_kernel,
        [(shape, F32)] + [(shape, BF16)] * 3,
        product,
        *theirs,
        weight,
        scratch=[pltpu.VMEM((2 * half, cols), F32)],
        limit=4,
        flops=flops,
    )


def over_x_kernel(total, one, two, three, kept, sent):
    half = total.shape[0] // NL
    for i, out in ((1, sent), (0, kept)):
        rows = slice(i * half, (i + 1) * half)
        value = total[rows, :] + one[rows, :].astype(F32)
        value = value + two[rows, :].astype(F32) + three[rows, :].astype(F32)
        out[...] = value.astype(out.dtype)


def local(tokens, gate_payload, gate_scales, up_payload, up_scales, down_payload, down_scales):
    count = tokens.shape[0] * NL * NX
    gate = weights(gate_payload, gate_scales, 4)
    (order,) = local_call(order_kernel, [((count, count), BF16)])
    pair = after(join(tokens, move_gy(tokens, dl=1)), gate, order)
    up = weights(after(up_payload, pair), up_scales, 4)
    two, one, three = move_gy(pair, dx=2), move_gy(pair, dx=1), move_gy(pair, dx=3)
    pieces = [pair, one, two, after(three, up)]

    depth, cols = gate.shape[0], 2 * gate.shape[1]
    rows = count // NC
    flops = 2 * rows * depth * cols
    features, sent = local_call(
        sent_kernel,
        [((rows, depth), BF16), ((rows, cols), BF16)],
        *pieces,
        order,
        gate,
        up,
        flops=flops,
    )
    received = move_gx(sent, dc=1)
    (kept,) = local_call(kept_kernel, [((rows, cols), F32)], features, gate, up, flops=flops)

    step = (rows // 8, cols)
    far0, far1, next1, back0 = local_call(leave_kernel, [(step, BF16)] * 4, kept, received)
    relay0, relay1 = move_gx(far0, dy=1), move_gx(far1, dy=-1)
    direct1, direct0 = move_gx(next1, dy=1), move_gx(back0, dy=-1)
    (through1,) = local_call(
        lambda *refs: relay_kernel(7, *refs), [(step, BF16)], kept, received, relay1
    )
    (through0,) = local_call(
        lambda *refs: relay_kernel(2, *refs), [(step, BF16)], kept, received, after(relay0, through1)
    )
    down = weights(after(down_payload, through0), down_scales.T, 13, flipped=True)
    through1, through0 = move_gx(through1, dy=-1), move_gx(through0, dy=1)
    units = cols // 2
    piece = (2 * ROWS, units)
    kept = after(kept, down)
    two, three = local_call(
        lambda *refs: over_y_kernel(1, *refs),
        [(piece, BF16)] * 2,
        kept,
        received,
        direct1,
        through1,
    )
    two = move_gx(two, dz=2)
    mine, one = local_call(
        lambda *refs: over_y_kernel(0, *refs),
        [(piece, F32), (piece, BF16)],
        kept,
        received,
        direct0,
        through0,
    )
    one, three = move_gx(one, dz=1), move_gx(three, dz=3)
    (hidden,) = local_call(hidden_kernel, [((ROWS, units), BF16)], mine, one, two, three)

    two, one, three = move_gx(hidden, dz=-2), move_gx(hidden, dz=-1), move_gx(hidden, dz=-3)
    one, three = first_awaited(two, one, three)
    (hidden,) = local_call(rows_kernel, [((NZ * ROWS, units), BF16)], hidden, one, two, three)
    two, one, three = move_gx(hidden, dy=-2), move_gx(hidden, dy=-1), move_gx(hidden, dy=-3)
    mine = [hidden, one, two, three]
    theirs = [move_gx(hidden, dc=1)]
    theirs += [move_gx(block, dc=1) for block in mine[1:]]
    total, one, two, three = last_products(mine, theirs, down)

    two, one, three = move_gy(two, dx=-2), move_gy(one, dx=-1), move_gy(three, dx=-3)
    one, three = first_awaited(two, one, three)
    shape = (total.shape[0] // NL, total.shape[1])
    total, sent = local_call(over_x_kernel, [(shape, F32), (shape, BF16)], total, one, two, three)
    return (total + move_gy(sent, dl=1).astype(F32)).astype(BF16)


def solution(mesh):
    placed = (
        P("gy", "gx"),
        P("gx", "gy"),
        P("gx", "gy"),
        P("gx", "gy"),
        P("gx", "gy"),
        P("gy", "gx"),
        P("gy", "gx"),
    )
    return jax.shard_map(
        local, mesh=mesh, in_specs=placed, out_specs=P("gy", "gx"), check_vma=False
    )
```

```python
import jax
import jax.numpy as jnp
from jax import lax
from jax.experimental import pallas as pl
from jax.experimental.pallas import tpu as pltpu
from jax.sharding import PartitionSpec as P

BLOCK = 128
F32 = jnp.float32
BF16 = jnp.bfloat16
NZ, NY, NC, NL, NX = 4, 4, 2, 2, 4
ROWS = 8
VMEM = pl.BlockSpec(memory_space=pltpu.VMEM)
HBM = pl.BlockSpec(memory_space=pltpu.HBM)
MIB = 2**20


def move_gx(x, dz=0, dy=0, dc=0):
    pairs = []
    for z in range(NZ):
        for y in range(NY):
            for c in range(NC):
                src = (z * NY + y) * NC + c
                dst = (((z + dz) % NZ) * NY + (y + dy) % NY) * NC + (c + dc) % NC
                pairs.append((src, dst))
    return lax.ppermute(x, "gx", pairs)


def move_gy(x, dl=0, dx=0):
    pairs = []
    for l in range(NL):
        for i in range(NX):
            pairs.append((l * NX + i, (l + dl) % NL * NX + (i + dx) % NX))
    return lax.ppermute(x, "gy", pairs)


def after(x, *others):
    return lax.optimization_barrier((x, *others))[0]


def in_vmem(x):
    return pltpu.with_memory_space_constraint(x, pltpu.VMEM)


def local_call(kernel, outs, *arrays, scratch=(), limit=2, flops=0):
    moved = sum(a.size * a.dtype.itemsize for a in arrays)
    return pl.pallas_call(
        kernel,
        in_specs=[VMEM] * len(arrays),
        out_specs=[VMEM] * len(outs),
        out_shape=[pltpu.VMEM(shape, dtype) for shape, dtype in outs],
        scratch_shapes=list(scratch),
        compiler_params=pltpu.CompilerParams(vmem_limit_bytes=limit * MIB),
        cost_estimate=pl.CostEstimate(flops=flops, bytes_accessed=moved, transcendentals=0),
    )(*[in_vmem(a) for a in arrays])


def weights_kernel(steps, flipped, payload, scales, out, held, factors, sems, sem):
    rows = payload.shape[0] // steps
    copies = [
        pltpu.make_async_copy(
            payload.at[pl.ds(i * rows, rows)], held.at[pl.ds(i * rows, rows)], sems.at[i]
        )
        for i in range(steps)
    ]
    small = pltpu.make_async_copy(scales, factors, sem)
    small.start()
    for copy in copies:
        copy.start()
    small.wait()
    for i, copy in enumerate(copies):
        copy.wait()
        for row in range(i * rows // BLOCK, (i + 1) * rows // BLOCK):
            for col in range(payload.shape[1] // BLOCK):
                at = (
                    slice(row * BLOCK, (row + 1) * BLOCK),
                    slice(col * BLOCK, (col + 1) * BLOCK),
                )
                factor = factors[col, row] if flipped else factors[row, col]
                out[at] = (held[at].astype(F32) * factor).astype(BF16)


def in_hbm(x):
    return pltpu.with_memory_space_constraint(x, pltpu.HBM)


def weights(payload, scales, steps, flipped=False):
    rows, cols = payload.shape
    return pl.pallas_call(
        lambda *refs: weights_kernel(steps, flipped, *refs),
        in_specs=[HBM, HBM],
        out_specs=VMEM,
        out_shape=pltpu.VMEM((rows, cols), BF16),
        scratch_shapes=[
            pltpu.VMEM((rows, cols), BF16),
            pltpu.SMEM(scales.shape, F32),
            pltpu.SemaphoreType.DMA((steps,)),
            pltpu.SemaphoreType.DMA,
        ],
        compiler_params=pltpu.CompilerParams(vmem_limit_bytes=5 * MIB),
        cost_estimate=pl.CostEstimate(
            flops=rows * cols, bytes_accessed=4 * rows * cols, transcendentals=0
        ),
    )(in_hbm(payload), in_hbm(scales))


def join_kernel(*refs):
    *pieces, out = refs
    at = 0
    for piece in pieces:
        rows = piece.shape[0]
        out[at : at + rows, :] = piece[...]
        at += rows


def join(*pieces):
    shape = (sum(p.shape[0] for p in pieces), pieces[0].shape[1])
    return local_call(join_kernel, [(shape, BF16)], *pieces)[0]


def position():
    index = lax.axis_index("gx")
    return index % NC, index // NC % NY, index // (NY * NC)


def order_kernel(out):
    where = position()
    step = 2 * ROWS
    for at in range(0, out.shape[0], step):
        row = lax.broadcasted_iota(jnp.int32, (step, out.shape[1]), 0)
        column = lax.broadcasted_iota(jnp.int32, (step, out.shape[1]), 1)
        first, second = (turned_row(at // ROWS + i, where) for i in (0, 1))
        chosen = jnp.where(row < ROWS, first, second - ROWS) + row
        out[at : at + step, :] = jnp.where(chosen == column, 1.0, 0.0).astype(BF16)


def turned_row(place, where):
    c, y, z = place // (NY * NZ), place // NZ % NY, place % NZ
    c, y, z = (where[0] + c) % NC, (where[1] + y) % NY, (where[2] + z) % NZ
    return pl.multiple_of(((c * NY + y) * NZ + z) * ROWS, ROWS)


def products(features, gate, up):
    width = gate.shape[1]
    for number, weight in ((0, gate), (1, up)):
        for col in range(0, width, 2 * BLOCK):
            out = slice(number * width + col, number * width + col + 2 * BLOCK)
            yield out, jnp.dot(
                features, weight[:, col : col + 2 * BLOCK], preferred_element_type=F32
            )


def sent_kernel(*refs):
    *pieces, order, gate, up, mine, sent = refs
    rows = jnp.concatenate([piece[...] for piece in pieces], axis=0)
    features = jnp.dot(order[...], rows, preferred_element_type=F32).astype(BF16)
    half = order.shape[0] // NC
    mine[...] = features[:half]
    for out, product in products(features[half:], gate, up):
        sent[:, out] = product.astype(BF16)


def kept_kernel(features, gate, up, kept):
    for out, product in products(features[...], gate, up):
        kept[:, out] = product


def columns(width, step):
    return [slice(i, i + step) for i in range(0, width, step)]


def over_columns(width, step, body):
    @pl.loop(0, width // step)
    def _(i):
        body(pl.multiple_of(i * step, step))


def summed(kept, received, part, cols):
    step = kept.shape[0] // 8
    rows = slice(part * step, (part + 1) * step)
    return kept[rows, cols] + received[rows, cols].astype(F32)


def leave_kernel(kept, received, far0, far1, next1, back0):
    def body(at):
        cols = pl.ds(at, 13 * BLOCK)
        for part, out in ((4, far0), (5, far1), (3, next1), (6, back0)):
            out[:, cols] = summed(kept, received, part, cols).astype(BF16)

    over_columns(kept.shape[1], 13 * BLOCK, body)


def relay_kernel(part, kept, received, relay, through):
    def body(at):
        cols = pl.ds(at, 13 * BLOCK)
        value = summed(kept, received, part, cols) + relay[:, cols].astype(F32)
        through[:, cols] = value.astype(BF16)

    over_columns(kept.shape[1], 13 * BLOCK, body)


def over_y_kernel(part, kept, received, direct, through, first, second):
    width = kept.shape[1] // 2

    def body(at):
        values = []
        for place in (0, width):
            cols = pl.ds(pl.multiple_of(place + at, BLOCK), 13 * BLOCK)
            value = summed(kept, received, part, cols)
            values.append(value + direct[:, cols].astype(F32) + through[:, cols].astype(F32))
        for i, out in enumerate((first, second)):
            both = jnp.concatenate([v[i * ROWS : (i + 1) * ROWS] for v in values], axis=0)
            out[:, pl.ds(at, 13 * BLOCK)] = both.astype(out.dtype)

    over_columns(width, 13 * BLOCK, body)


def hidden_kernel(mine, one, two, three, hidden):
    for cols in columns(hidden.shape[1], 2 * BLOCK):
        total = mine[:, cols] + one[:, cols].astype(F32)
        total = total + two[:, cols].astype(F32) + three[:, cols].astype(F32)
        hidden[:, cols] = (jax.nn.silu(total[:ROWS]) * total[ROWS:]).astype(BF16)


def corner_kernel(x, out):
    out[...] = x[: out.shape[0], : out.shape[1]]


def rows_kernel(a, b, c, d, out):
    for i, pair in ((0, (a, b)), (2, (c, d))):
        for cols in columns(out.shape[1], 2 * BLOCK):
            value = jnp.concatenate([piece[:, cols].astype(F32) for piece in pair], axis=0)
            out[i * ROWS : (i + 2) * ROWS, cols] = value.astype(BF16)


def mine_kernel(*refs):
    *hidden, weight, out = refs
    rows = jnp.concatenate([piece[...] for piece in hidden], axis=0)
    out[...] = jnp.dot(rows, weight[...], preferred_element_type=F32)


def last_kernel(mine, *refs):
    where = position()
    *hidden, weight, kept, one, two, three, terms = refs
    half = mine.shape[0]
    rows = jnp.concatenate([piece[...] for piece in hidden], axis=0)
    for place in range(half // ROWS):
        terms[pl.ds(turned_row(place, where), ROWS), :] = mine[place * ROWS : (place + 1) * ROWS, :]
    product = jnp.dot(rows, weight[...], preferred_element_type=F32)
    for place in range(half // ROWS):
        terms[pl.ds(turned_row(half // ROWS + place, where), ROWS), :] = product[
            place * ROWS : (place + 1) * ROWS
        ]
    for i, out in enumerate((kept, one, two, three)):
        rows = slice(i * 2 * half // NX, (i + 1) * 2 * half // NX)
        out[...] = terms[rows, :].astype(out.dtype)


def last_products(mine, theirs, weight):
    half = sum(p.shape[0] for p in mine)
    depth, cols = weight.shape
    flops = 2 * half * depth * cols
    (product,) = local_call(mine_kernel, [((half, cols), F32)], *mine, weight, flops=flops)
    shape = (2 * half // NX, cols)
    return local_call(
        last_kernel,
        [(shape, F32)] + [(shape, BF16)] * 3,
        product,
        *theirs,
        weight,
        scratch=[pltpu.VMEM((2 * half, cols), F32)],
        limit=4,
        flops=flops,
    )


def over_x_kernel(total, one, two, three, kept, sent):
    half = total.shape[0] // NL
    for i, out in ((1, sent), (0, kept)):
        rows = slice(i * half, (i + 1) * half)
        value = total[rows, :] + one[rows, :].astype(F32)
        value = value + two[rows, :].astype(F32) + three[rows, :].astype(F32)
        out[...] = value.astype(out.dtype)


def local(tokens, gate_payload, gate_scales, up_payload, up_scales, down_payload, down_scales):
    count = tokens.shape[0] * NL * NX
    gate = weights(gate_payload, gate_scales, 4)
    (order,) = local_call(order_kernel, [((count, count), BF16)])
    pair = after(join(tokens, move_gy(tokens, dl=1)), gate, order)
    up = weights(after(up_payload, pair), up_scales, 4)
    two, one, three = move_gy(pair, dx=2), move_gy(pair, dx=1), move_gy(pair, dx=3)
    pieces = [pair, one, two, after(three, up)]

    depth, cols = gate.shape[0], 2 * gate.shape[1]
    rows = count // NC
    flops = 2 * rows * depth * cols
    features, sent = local_call(
        sent_kernel,
        [((rows, depth), BF16), ((rows, cols), BF16)],
        *pieces,
        order,
        gate,
        up,
        flops=flops,
    )
    received = move_gx(sent, dc=1)
    (kept,) = local_call(kept_kernel, [((rows, cols), F32)], features, gate, up, flops=flops)

    step = (rows // 8, cols)
    far0, far1, next1, back0 = local_call(leave_kernel, [(step, BF16)] * 4, kept, received)
    relay0, relay1 = move_gx(far0, dy=1), move_gx(far1, dy=-1)
    direct1, direct0 = move_gx(next1, dy=1), move_gx(back0, dy=-1)
    (through1,) = local_call(
        lambda *refs: relay_kernel(7, *refs), [(step, BF16)], kept, received, relay1
    )
    (through0,) = local_call(
        lambda *refs: relay_kernel(2, *refs), [(step, BF16)], kept, received, after(relay0, through1)
    )
    down = weights(after(down_payload, through0), down_scales.T, 13, flipped=True)
    through1, through0 = move_gx(through1, dy=-1), move_gx(through0, dy=1)
    units = cols // 2
    piece = (2 * ROWS, units)
    kept = after(kept, down)
    two, three = local_call(
        lambda *refs: over_y_kernel(1, *refs),
        [(piece, BF16)] * 2,
        kept,
        received,
        direct1,
        through1,
    )
    two = move_gx(two, dz=2)
    mine, one = local_call(
        lambda *refs: over_y_kernel(0, *refs),
        [(piece, F32), (piece, BF16)],
        kept,
        received,
        direct0,
        through0,
    )
    one, three = move_gx(one, dz=1), move_gx(three, dz=3)
    (hidden,) = local_call(hidden_kernel, [((ROWS, units), BF16)], mine, one, two, three)

    two, one, three = move_gx(hidden, dz=-2), move_gx(hidden, dz=-1), move_gx(hidden, dz=-3)
    (hidden,) = local_call(rows_kernel, [((NZ * ROWS, units), BF16)], hidden, one, two, three)
    two, one, three = move_gx(hidden, dy=-2), move_gx(hidden, dy=-1), move_gx(hidden, dy=-3)
    (corner,) = local_call(corner_kernel, [((8, BLOCK), BF16)], two)
    one, three = after(one, corner), after(three, corner)
    mine = [hidden, one, two, three]
    theirs = [move_gx(hidden, dc=1)]
    theirs += [move_gx(block, dc=1) for block in mine[1:]]
    total, one, two, three = last_products(mine, theirs, down)

    two, one, three = move_gy(two, dx=-2), move_gy(one, dx=-1), move_gy(three, dx=-3)
    shape = (total.shape[0] // NL, total.shape[1])
    total, sent = local_call(over_x_kernel, [(shape, F32), (shape, BF16)], total, one, two, three)
    return (total + move_gy(sent, dl=1).astype(F32)).astype(BF16)


def solution(mesh):
    placed = (
        P("gy", "gx"),
        P("gx", "gy"),
        P("gx", "gy"),
        P("gx", "gy"),
        P("gx", "gy"),
        P("gy", "gx"),
        P("gy", "gx"),
    )
    return jax.shard_map(
        local, mesh=mesh, in_specs=placed, out_specs=P("gy", "gx"), check_vma=False
    )
```
